32 devices in a mesh: pair: 16 (over z, y, x), int: 2 (over core).
Axes of the slice: x: 2, y: 2, z: 4, core: 2. Of those that a mesh axis runs over, the one named last changes fastest.
Arguments:
- amps: bfloat16 [128, 64, 4096], P('pair', None, 'int'), may hold values from -6 to 6
- amp_mask: int32 [128, 64], P('pair'), may hold values 0 or 1
- integrals: bfloat16 [64, 4096, 4096], P('pair', None, 'int'), may hold values from -0.09375 to 0.09375
- block_mask: int32 [64], P('pair'), may hold values 0 or 1
- in_tiles: int32 [64], replicated, may hold values from 0 to 63, each once
- out_tiles: int32 [64], replicated, may hold values from 0 to 63, each once
- vir_energy: float32 [1024], replicated, may hold values from 0.5 to 3
- pair_energy: float32 [128], P('pair'), may hold values from -4 to -1
- dressing: bfloat16 [1024, 1024], P('pair'), may hold values from -0.1875 to 0.1875
Outputs:
- new_amps: bfloat16 [128, 64, 4096], P('pair', None, 'int')
The draws below stay inside these ranges and needn't reach their ends.
Inputs may be any that keep to these rules, and one draw needn't show every extreme that they name: `in_tiles`: a permutation of the 64 tiles. `out_tiles`: a permutation of the 64 tiles.
All inputs are finite; a program needn't handle non-finite values. No bound on the sum of `amp_mask` or of `block_mask` on one device may be relied on, other than what follows from the above.
Results may differ from the reference program's by a relative error of at most 0.0038.
Values may be sent and summed in bfloat16 or wider, within the bound.
No kernel may reach another device: no remote copies, remote signals or barrier semaphores. Data moves between devices by JAX's collectives and lax.ppermute only.
A program may use at most 192 MiB of HBM per device.

```python
import jax
import jax.numpy as jnp
from jax import lax

TILE = 64
VT = 16
WA = 4
P_SIZE = 128
NPT = 64
TE = 4096
NV = 1024
N_INT = 2


def place_ends(array, key, smallest, largest):
    longest = array.shape.index(max(array.shape))
    spots = []
    for shift in (0, 1):
        where = [jax.random.randint(jax.random.fold_in(key, axis), (), 0, length) for axis, length in enumerate(array.shape)]
        where[longest] = (where[longest] + shift) % array.shape[longest]
        spots.append(tuple(where))
    return array.at[spots[0]].set(smallest).at[spots[1]].set(largest)


def level_of(own_key, shape, pieces, least, top_value):
    level, own = 1.0, jax.random.fold_in(own_key, 6)
    for position, parts in pieces:
        steps = jnp.exp(jax.random.uniform(jax.random.fold_in(own, position), (parts,), jnp.float32, least / len(pieces), top_value / len(pieces)))
        level = level * jnp.repeat(steps, shape[position] // parts).reshape([-1 if axis == position else 1 for axis in range(len(shape))])
    return level


def gaussian(rng, dims, scale, reach, split=(), kind=jnp.bfloat16):
    result = scale * jax.random.normal(rng, dims, jnp.float32)
    if split:
        result = result * level_of(rng, dims, split, -0.22, 0.18)
    return jnp.clip(result, -reach, reach).astype(kind)


def setup_inputs(seed: int = 0) -> dict:
    splits = jax.random.split(jax.random.key(seed), 10)
    return {
        "amps": gaussian(splits[0], (P_SIZE, NPT, TE), 1.0, 6.0, ((0, 16), (2, 2))),
        "amp_mask": place_ends((jax.random.randint(splits[1], (P_SIZE, NPT), 0, 4) < 3).astype(jnp.int32), jax.random.fold_in(splits[1], 1), 0, 1),
        "integrals": gaussian(splits[2], (NPT, TE, TE), TE ** -0.5, 0.09375, ((0, 16), (2, 2))),
        "block_mask": place_ends((jax.random.randint(splits[3], (NPT,), 0, 4) < 3).astype(jnp.int32), jax.random.fold_in(splits[3], 1), 0, 1),
        "in_tiles": jax.random.permutation(splits[4], NPT).astype(jnp.int32),
        "out_tiles": jax.random.permutation(splits[5], NPT).astype(jnp.int32),
        "vir_energy": jnp.clip(jax.random.uniform(splits[6], (NV,), jnp.float32, 0.5, 3.0), 0.5, 3.0),
        "pair_energy": jnp.clip(-4.0 + 3.0 * jax.random.uniform(splits[7], (P_SIZE,), jnp.float32) ** level_of(splits[7], (P_SIZE,), ((0, 16),), -0.2, 0.2), -4.0, -1.0),
        "dressing": gaussian(splits[8], (NV, NV), NV ** -0.5, 0.1875, ((0, 16),)),
    }


def reference(amps, amp_mask, integrals, block_mask, in_tiles, out_tiles, vir_energy, pair_energy, dressing):
    pair_count = amps.shape[0]
    tile_count = amps.shape[1]
    tile_entries = amps.shape[2]
    group_size = tile_entries // N_INT
    masked = jnp.where(amp_mask[:, :, None] > 0, amps, jnp.zeros_like(amps))

    def one_slot(slot_args):
        integral_block, source, keep_block = slot_args
        amp_rows = jnp.take(masked, source.astype(jnp.int32), axis=1).astype(jnp.float32)
        amp_rows = amp_rows.reshape(pair_count, N_INT, group_size)
        block_wide = integral_block.astype(jnp.float32).reshape(tile_entries, N_INT, group_size)
        int_parts = jnp.einsum("pnk,ank->npa", amp_rows, block_wide)
        int_parts = int_parts * keep_block.astype(jnp.float32)
        int_parts = lax.optimization_barrier(int_parts.astype(jnp.bfloat16)).astype(jnp.float32)
        return jnp.sum(int_parts, axis=0)

    ladder_slots = lax.map(one_slot, (integrals, in_tiles, block_mask))
    slot_of = jnp.zeros((tile_count,), jnp.int32).at[out_tiles.astype(jnp.int32)].set(jnp.arange(tile_count, dtype=jnp.int32))
    ladder = jnp.transpose(jnp.take(ladder_slots, slot_of, axis=0), (1, 0, 2))

    amp_grid = masked.reshape(pair_count, WA, VT, TILE, TILE).astype(jnp.float32)
    dress_grid = dressing.reshape(VT, TILE, VT, TILE).astype(jnp.float32)
    cycle = jnp.einsum("pxyuv,yvzw->pxzuw", amp_grid, dress_grid).reshape(pair_count, tile_count, tile_entries)

    energies = vir_energy.reshape(VT, TILE)
    first_energy = energies[:WA]
    denominator = pair_energy[:, None, None, None, None] - first_energy[None, :, None, :, None] - energies[None, None, :, None, :]
    denominator = denominator.reshape(pair_count, tile_count, tile_entries)
    updated = masked.astype(jnp.float32) + (ladder + cycle) / denominator
    return updated.astype(jnp.bfloat16)
```

```python
import jax
import jax.numpy as jnp
from jax import lax
from jax.experimental import pallas as pl
from jax.experimental.pallas import tpu as pltpu
from jax.sharding import PartitionSpec as P

TILE = 64
VT = 16
WA = 4
LANES = 128
MIB = 1 << 20


def prepare_kernel(owners, in_tiles_ref, amps_ref, mask_ref, tiles_ref, *sent_refs):
    tile_count = amps_ref.shape[1]
    swapped = jnp.swapaxes(amps_ref[...].astype(jnp.float32), 0, 1)
    for tile in range(tile_count):
        kept = jnp.where(mask_ref[:, tile : tile + 1] > 0, swapped[tile], 0.0)
        tiles_ref[tile] = kept.astype(tiles_ref.dtype)
    size = tile_count // owners // len(sent_refs)
    for chunk, sent_ref in enumerate(sent_refs):
        for owner in range(owners):
            for slot in range(size):
                source = in_tiles_ref[(owner * len(sent_refs) + chunk) * size + slot]
                sent_ref[owner, slot] = tiles_ref[source]


def prepare(in_tiles, amps, amp_mask, owners, chunks):
    pairs, tiles, share = amps.shape
    width = min(share, 1024)
    size = tiles // owners // chunks
    return pl.pallas_call(
        lambda *refs: prepare_kernel(owners, *refs),
        out_shape=(jax.ShapeDtypeStruct((tiles, pairs, share), amps.dtype),)
        + (jax.ShapeDtypeStruct((owners, size, pairs, share), amps.dtype),) * chunks,
        grid_spec=pltpu.PrefetchScalarGridSpec(
            num_scalar_prefetch=1,
            grid=(share // width,),
            in_specs=[
                pl.BlockSpec((pairs, tiles, width), lambda i, _: (0, 0, i)),
                pl.BlockSpec((pairs, tiles), lambda i, _: (0, 0)),
            ],
            out_specs=[pl.BlockSpec((tiles, pairs, width), lambda i, _: (0, 0, i))]
            + [pl.BlockSpec((owners, size, pairs, width), lambda i, _: (0, 0, 0, i))] * chunks,
        ),
        compiler_params=pltpu.CompilerParams(vmem_limit_bytes=56 * MIB),
        cost_estimate=pl.CostEstimate(
            flops=2 * pairs * tiles * share,
            bytes_accessed=6 * pairs * tiles * share,
            transcendentals=0,
        ),
    )(in_tiles, amps, amp_mask)


def ladder_kernel(first_slot, index_ref, keep_ref, x_ref, w_ref, *rest):
    out_refs, x_rows = rest[:-1], rest[-1]
    part, slot, block = pl.program_id(0), pl.program_id(1), pl.program_id(2)
    rows, depth = x_rows.shape

    @pl.when(block == 0)
    def _():
        x = x_ref[:, 0].astype(jnp.float32).reshape(rows, depth)
        x_rows[...] = x.astype(x_rows.dtype)

    keep = keep_ref[first_slot + slot] > 0
    product = lax.dot_general(
        x_rows[...], w_ref[0], (((1,), (1,)), ((), ())), preferred_element_type=jnp.float32
    )
    product = jnp.where(keep, product, 0.0)
    for index, out_ref in enumerate(out_refs):

        @pl.when(part == index)
        def _():
            shape = (out_ref.shape[0], out_ref.shape[2], out_ref.shape[3])
            out_ref[:, 0] = product.reshape(shape).astype(out_ref.dtype)


def ladder(int_index, block_mask, received, integrals, chunk, parts):
    owners, chunk_slots, pairs, depth = received.shape
    entries = integrals.shape[1]
    share = entries // parts
    width = min(share, 2048)
    blocks = share // width
    first_slot = chunk * chunk_slots

    def block_of(part, block, index_ref):
        return lax.rem(index_ref[0] + 1 + part, parts) * blocks + block

    def out_map(index):
        def where(part, slot, block, index_ref, keep_ref):
            at = lambda value, last: jnp.where(
                part == index, value, jnp.where(part < index, 0, last)
            )
            return (0, at(slot, chunk_slots - 1), 0, at(block, blocks - 1))

        return where

    return pl.pallas_call(
        lambda *refs: ladder_kernel(first_slot, *refs),
        out_shape=tuple(
            jax.ShapeDtypeStruct((owners, chunk_slots, pairs, share), received.dtype)
            for _ in range(parts)
        ),
        grid_spec=pltpu.PrefetchScalarGridSpec(
            num_scalar_prefetch=2,
            grid=(parts, chunk_slots, blocks),
            in_specs=[
                pl.BlockSpec((owners, 1, pairs, depth), lambda h, s, b, i, k: (0, s, 0, 0)),
                pl.BlockSpec(
                    (1, width, depth), lambda h, s, b, i, k: (first_slot + s, block_of(h, b, i), 0)
                ),
            ],
            out_specs=[
                pl.BlockSpec((owners, 1, pairs, width), out_map(index)) for index in range(parts)
            ],
            scratch_shapes=[pltpu.VMEM((owners * pairs, depth), received.dtype)],
        ),
        compiler_params=pltpu.CompilerParams(vmem_limit_bytes=24 * MIB),
        cost_estimate=pl.CostEstimate(
            flops=2 * owners * pairs * chunk_slots * entries * depth,
            bytes_accessed=2 * chunk_slots * entries * depth,
            transcendentals=0,
        ),
    )(int_index, block_mask, received, integrals)


def cycle_kernel(
    owners, parts, place_ref, tiles_ref, first_ref, second_ref, energy_ref, *rest
):
    pieces, (base_ref, dress, wide, rows) = rest[:-4], rest[-4:]
    groups = tiles_ref.shape[2] // LANES
    pairs = tiles_ref.shape[1]
    outer_tile = pl.program_id(0)

    @pl.when(outer_tile == 0)
    def _():
        own = pieces[0].shape[2]
        for owner in range(owners):
            for part in range(parts):
                away = place_ref[1] ^ part
                source = place_ref[0] ^ owner
                block = pieces[0][lax.div(away, len(pieces)), source].astype(jnp.float32)
                for index in range(1, len(pieces)):
                    other = pieces[index][lax.div(away, len(pieces)), source].astype(jnp.float32)
                    block = jnp.where(lax.rem(away, len(pieces)) == index, other, block)
                start = (owner * parts + part) * own
                dress[start : start + own] = block
        low = lax.broadcasted_iota(jnp.int32, (TILE, LANES), 1) < TILE
        for inner in range(VT):
            for couple in range(VT // 2):
                block = dress[
                    inner * TILE : (inner + 1) * TILE, couple * LANES : (couple + 1) * LANES
                ]
                turned = pltpu.roll(block, TILE, 1)
                even = slice(2 * couple * LANES, (2 * couple + 1) * LANES)
                odd = slice((2 * couple + 1) * LANES, (2 * couple + 2) * LANES)
                upper = slice(inner * LANES, inner * LANES + TILE)
                lower = slice(inner * LANES + TILE, (inner + 1) * LANES)
                wide[upper, even] = jnp.where(low, block, 0.0).astype(wide.dtype)
                wide[upper, odd] = jnp.where(low, turned, 0.0).astype(wide.dtype)
                wide[lower, even] = jnp.where(low, 0.0, turned).astype(wide.dtype)
                wide[lower, odd] = jnp.where(low, 0.0, block).astype(wide.dtype)

    for inner in range(VT):
        tile = tiles_ref[inner].astype(jnp.float32)
        stacked = jnp.concatenate(
            [tile[:, g * LANES : (g + 1) * LANES] for g in range(groups)], axis=0
        )
        rows[:, inner * LANES : (inner + 1) * LANES] = stacked.astype(rows.dtype)
    for outer in range(0, VT, 2):
        span = slice(outer * LANES, (outer + 2) * LANES)
        product = jnp.dot(rows[...], wide[:, span], preferred_element_type=jnp.float32)
        for half in range(2):
            cycle = jnp.concatenate(
                [
                    product[g * pairs : (g + 1) * pairs, half * LANES : (half + 1) * LANES]
                    for g in range(groups)
                ],
                axis=1,
            )
            b = outer + half
            below = energy_ref[...] - first_ref[0] - second_ref[b]
            base_ref[b] = tiles_ref[b].astype(jnp.float32) + cycle / below


def cycle_terms(place, tiles, first, second, pair_energy, pieces, owners, parts):
    count, pairs, share = tiles.shape
    whole = lambda a: pl.BlockSpec(a.shape, lambda i, *_: (0,) * a.ndim)
    return pl.pallas_call(
        lambda *refs: cycle_kernel(owners, parts, *refs),
        out_shape=jax.ShapeDtypeStruct(tiles.shape, jnp.float32),
        grid_spec=pltpu.PrefetchScalarGridSpec(
            num_scalar_prefetch=1,
            grid=(WA,),
            in_specs=[
                pl.BlockSpec((VT, pairs, share), lambda i, *_: (i, 0, 0)),
                pl.BlockSpec((1, 1, share), lambda i, *_: (i, 0, 0)),
                whole(second),
                whole(pair_energy),
            ]
            + [whole(piece) for piece in pieces],
            out_specs=pl.BlockSpec((VT, pairs, share), lambda i, *_: (i, 0, 0)),
            scratch_shapes=[
                pltpu.VMEM((VT * TILE, VT * TILE), jnp.float32),
                pltpu.VMEM((VT * LANES, VT * LANES), tiles.dtype),
                pltpu.VMEM((pairs * share // LANES, VT * LANES), tiles.dtype),
            ],
        ),
        compiler_params=pltpu.CompilerParams(vmem_limit_bytes=48 * MIB),
        cost_estimate=pl.CostEstimate(
            flops=4 * count * pairs * share * VT * TILE,
            bytes_accessed=8 * count * pairs * share,
            transcendentals=0,
        ),
    )(place, tiles, first, second, pair_energy, *pieces)


def finish_kernel(
    chunks, out_tiles_ref, base_ref, first_ref, second_ref, energy_ref, *rest
):
    parts, out_ref, sums = rest[:chunks], rest[-2], rest[-1]
    for chunk, part in enumerate(parts):
        owners, size = part.shape[:2]
        for owner in range(owners):
            for slot in range(size):
                tile = out_tiles_ref[(owner * chunks + chunk) * size + slot]
                below = (
                    energy_ref[...] - first_ref[lax.div(tile, VT)] - second_ref[lax.rem(tile, VT)]
                )
                sums[tile] = base_ref[tile] + part[owner, slot].astype(jnp.float32) / below
    out_ref[...] = jnp.swapaxes(sums[...], 0, 1).astype(out_ref.dtype)


def finish(out_tiles, base, first, second, pair_energy, parts, dtype):
    count, pairs, share = base.shape
    width = min(share, 512)
    return pl.pallas_call(
        lambda *refs: finish_kernel(len(parts), *refs),
        out_shape=jax.ShapeDtypeStruct((pairs, count, share), dtype),
        grid_spec=pltpu.PrefetchScalarGridSpec(
            num_scalar_prefetch=1,
            grid=(share // width,),
            in_specs=[
                pl.BlockSpec((count, pairs, width), lambda i, _: (0, 0, i)),
                pl.BlockSpec((WA, 1, width), lambda i, _: (0, 0, i)),
                pl.BlockSpec((VT, 1, width), lambda i, _: (0, 0, i)),
                pl.BlockSpec((pairs, 1), lambda i, _: (0, 0)),
            ]
            + [
                pl.BlockSpec(part.shape[:2] + (pairs, width), lambda i, _: (0, 0, 0, i))
                for part in parts
            ],
            out_specs=pl.BlockSpec((pairs, count, width), lambda i, _: (0, 0, i)),
            scratch_shapes=[pltpu.VMEM((count, pairs, width), jnp.float32)],
        ),
        compiler_params=pltpu.CompilerParams(vmem_limit_bytes=56 * MIB),
        cost_estimate=pl.CostEstimate(
            flops=8 * count * pairs * share,
            bytes_accessed=8 * count * pairs * share,
            transcendentals=0,
        ),
    )(out_tiles, base, first, second, pair_energy, *parts)


def exchanges(axis, size, radices):
    steps, reach = [], size
    while reach > 1:
        radix = radices.pop(0) if radices else 4
        radix = radix if reach % radix == 0 else 2
        reach //= radix
        steps.append((axis, size, [reach * m for m in range(1, radix)]))
    return steps


def exchange(block, step):
    axis, size, distances = step
    others = [
        lax.ppermute(block, axis, [(j, j ^ distance) for j in range(size)])
        for distance in distances
    ]
    return [block, *others]


def joined(blocks):
    return jnp.stack(blocks, axis=1).reshape((-1,) + blocks[0].shape[1:])


def solution(mesh):
    owners, parts = mesh.shape["pair"], mesh.shape["int"]

    def shards(
        amps, amp_mask, integrals, block_mask, in_tiles, out_tiles, vir_energy, pair_energy, dressing
    ):
        pairs, tiles, share = amps.shape
        slots = tiles // owners
        chunks = 2 if slots % 2 == 0 else 1
        size = slots // chunks
        strip = share // TILE
        int_index = lax.axis_index("int")

        masked, *sent = prepare(in_tiles, amps, amp_mask, owners, chunks)

        def exchanged(part):
            return lax.all_to_all(part, "pair", split_axis=0, concat_axis=0, tiled=True)

        rows, columns = dressing.shape
        own = rows // parts
        steps = exchanges("pair", owners, [2, 2])
        gathered = [lax.dynamic_slice_in_dim(dressing, int_index * own, own, 0)[None]]
        together = lax.optimization_barrier
        received, returned = [], []
        for c in range(chunks):
            if c:
                received[-1], sent[c] = together((received[-1], sent[c]))
            received.append(exchanged(sent[c]))
        for c in range(chunks):
            if c == 0 and steps:
                gathered = exchange(joined(gathered), steps.pop(0))
            if c == 0:
                received[c], gathered = together((received[c], gathered))
            if steps:
                gathered = exchange(joined(gathered), steps.pop(0))
            terms = ladder(
                int_index.astype(jnp.int32)[None], block_mask, received[c], integrals, c, parts
            )
            (*others, total), gathered = together((terms, gathered))
            total = total.astype(jnp.float32)
            for r, other in enumerate(others):
                got = lax.ppermute(
                    other, "int", [(j, (j + 1 + r) % parts) for j in range(parts)]
                )
                total = total + got.astype(jnp.float32)
            total = total.astype(amps.dtype)
            if c == 0:
                received[-1], total = together((received[-1], total))
            else:
                returned[-1], total = together((returned[-1], total))
            returned.append(exchanged(total))

        while steps:
            gathered = exchange(joined(gathered), steps.pop(0))
        returned[0], gathered = together((returned[0], gathered))
        pieces = [joined(gathered)[None]]
        for step in exchanges("int", parts, []):
            pieces = exchange(joined(pieces), step)

        energies = vir_energy.reshape(VT, TILE)
        own_energy = lax.dynamic_slice_in_dim(energies[:WA], int_index * strip, strip, 1)
        first = jnp.repeat(own_energy, TILE, axis=1)[:, None]
        second = jnp.tile(energies, (1, strip))[:, None]
        energy = pair_energy[:, None]
        place = jnp.stack([lax.axis_index("pair"), int_index]).astype(jnp.int32)
        base = cycle_terms(place, masked, first, second, energy, pieces, owners, parts)
        return finish(out_tiles, base, first, second, energy, returned, amps.dtype)

    in_specs = (
        P("pair", None, "int"),
        P("pair", None),
        P("pair", None, "int"),
        P("pair"),
        P(),
        P(),
        P(),
        P("pair"),
        P("pair", None),
    )
    out_specs = P("pair", None, "int")
    return jax.shard_map(shards, mesh=mesh, in_specs=in_specs, out_specs=out_specs, check_vma=False)
```

```python
import jax
import jax.numpy as jnp
from jax import lax
from jax.experimental import pallas as pl
from jax.experimental.pallas import tpu as pltpu
from jax.sharding import PartitionSpec as P

TILE = 64
VT = 16
WA = 4
LANES = 128
MIB = 1 << 20


def selection(tile, tile_count, pairs):
    shape = (pairs, pairs * tile_count)
    column = lax.broadcasted_iota(jnp.int32, shape, 1)
    return column == lax.broadcasted_iota(jnp.int32, shape, 0) * tile_count + tile


def first_kernel(chunks, in_tiles_ref, amps_ref, mask_ref, sent_ref, picks):
    pairs, tile_count, width = amps_ref.shape
    owners, size = sent_ref.shape[:2]

    @pl.when(pl.program_id(0) == 0)
    def _():
        mask = jnp.concatenate([mask_ref[...]] * pairs, axis=1) > 0
        for owner in range(owners):
            for slot in range(size):
                tile = in_tiles_ref[owner * chunks * size + slot]
                row = (owner * size + slot) * pairs
                picked = selection(tile, tile_count, pairs) & mask
                picks[row : row + pairs] = jnp.where(picked, 1.0, 0.0)

    amps = amps_ref[...].reshape(pairs * tile_count, width)
    rows = jnp.dot(picks[...].astype(amps.dtype), amps, preferred_element_type=jnp.float32)
    sent_ref[...] = rows.reshape(sent_ref.shape).astype(sent_ref.dtype)


def prepare_first(in_tiles, amps, amp_mask, owners, chunks):
    pairs, tiles, share = amps.shape
    width = min(share, 1024)
    size = tiles // owners // chunks
    return pl.pallas_call(
        lambda *refs: first_kernel(chunks, *refs),
        out_shape=jax.ShapeDtypeStruct((owners, size, pairs, share), amps.dtype),
        grid_spec=pltpu.PrefetchScalarGridSpec(
            num_scalar_prefetch=1,
            grid=(share // width,),
            in_specs=[
                pl.BlockSpec((pairs, tiles, width), lambda i, _: (0, 0, i)),
                pl.BlockSpec((pairs, tiles), lambda i, _: (0, 0)),
            ],
            out_specs=pl.BlockSpec((owners, size, pairs, width), lambda i, _: (0, 0, 0, i)),
            scratch_shapes=[pltpu.VMEM((owners * size * pairs, pairs * tiles), jnp.float32)],
        ),
        compiler_params=pltpu.CompilerParams(vmem_limit_bytes=56 * MIB),
        cost_estimate=pl.CostEstimate(
            flops=2 * pairs * pairs * tiles * tiles * share // chunks,
            bytes_accessed=3 * pairs * tiles * share,
            transcendentals=0,
        ),
    )(in_tiles, amps, amp_mask)


def prepare_kernel(owners, chunks, in_tiles_ref, amps_ref, mask_ref, tiles_ref, *sent_refs):
    tile_count = amps_ref.shape[1]
    swapped = jnp.swapaxes(amps_ref[...].astype(jnp.float32), 0, 1)
    for tile in range(tile_count):
        kept = jnp.where(mask_ref[:, tile : tile + 1] > 0, swapped[tile], 0.0)
        tiles_ref[tile] = kept.astype(tiles_ref.dtype)
    size = tile_count // owners // chunks
    for chunk, sent_ref in enumerate(sent_refs, start=1):
        for owner in range(owners):
            for slot in range(size):
                source = in_tiles_ref[(owner * chunks + chunk) * size + slot]
                sent_ref[owner, slot] = tiles_ref[source]


def prepare(in_tiles, amps, amp_mask, owners, chunks):
    pairs, tiles, share = amps.shape
    width = min(share, 1024)
    size = tiles // owners // chunks
    return pl.pallas_call(
        lambda *refs: prepare_kernel(owners, chunks, *refs),
        out_shape=(jax.ShapeDtypeStruct((tiles, pairs, share), amps.dtype),)
        + (jax.ShapeDtypeStruct((owners, size, pairs, share), amps.dtype),) * (chunks - 1),
        grid_spec=pltpu.PrefetchScalarGridSpec(
            num_scalar_prefetch=1,
            grid=(share // width,),
            in_specs=[
                pl.BlockSpec((pairs, tiles, width), lambda i, _: (0, 0, i)),
                pl.BlockSpec((pairs, tiles), lambda i, _: (0, 0)),
            ],
            out_specs=[pl.BlockSpec((tiles, pairs, width), lambda i, _: (0, 0, i))]
            + [pl.BlockSpec((owners, size, pairs, width), lambda i, _: (0, 0, 0, i))]
            * (chunks - 1),
        ),
        compiler_params=pltpu.CompilerParams(vmem_limit_bytes=56 * MIB),
        cost_estimate=pl.CostEstimate(
            flops=2 * pairs * tiles * share,
            bytes_accessed=6 * pairs * tiles * share,
            transcendentals=0,
        ),
    )(in_tiles, amps, amp_mask)


def ladder_kernel(first_slot, index_ref, keep_ref, x_ref, w_ref, *rest):
    out_refs, (x_columns, sums) = rest[:-2], rest[-2:]
    part, slot, block = pl.program_id(0), pl.program_id(1), pl.program_id(2)
    depth, rows = x_columns.shape[1:]
    step = min(depth, 256)

    @pl.when((part == 0) & (block == 0))
    def _():
        x = x_ref[:, 0].astype(jnp.float32).reshape(rows, depth)
        x_columns[slot] = x.T.astype(x_columns.dtype)

    for k in range(0, depth, step):
        product = jnp.dot(
            w_ref[0, :, k : k + step],
            x_columns[slot, k : k + step],
            preferred_element_type=jnp.float32,
        )
        sums[...] = product if k == 0 else sums[...] + product
    keep = keep_ref[first_slot + slot] > 0
    product = jnp.where(keep, sums[...].T, 0.0)
    for index, out_ref in enumerate(out_refs):

        @pl.when(part == index)
        def _():
            shape = (out_ref.shape[0], out_ref.shape[2], out_ref.shape[3])
            out_ref[:, 0] = product.reshape(shape).astype(out_ref.dtype)


def ladder(int_index, block_mask, received, integrals, chunk, parts):
    owners, chunk_slots, pairs, depth = received.shape
    entries = integrals.shape[1]
    share = entries // parts
    width = min(share, 2048)
    blocks = share // width
    first_slot = chunk * chunk_slots

    def block_of(part, block, index_ref):
        return lax.rem(index_ref[0] + 1 + part, parts) * blocks + block

    def out_map(index):
        def where(part, slot, block, index_ref, keep_ref):
            at = lambda value, last: jnp.where(
                part == index, value, jnp.where(part < index, 0, last)
            )
            return (0, at(slot, chunk_slots - 1), 0, at(block, blocks - 1))

        return where

    return pl.pallas_call(
        lambda *refs: ladder_kernel(first_slot, *refs),
        out_shape=tuple(
            jax.ShapeDtypeStruct((owners, chunk_slots, pairs, share), received.dtype)
            for _ in range(parts)
        ),
        grid_spec=pltpu.PrefetchScalarGridSpec(
            num_scalar_prefetch=2,
            grid=(parts, chunk_slots, blocks),
            in_specs=[
                pl.BlockSpec((owners, 1, pairs, depth), lambda h, s, b, i, k: (0, s, 0, 0)),
                pl.BlockSpec(
                    (1, width, depth), lambda h, s, b, i, k: (first_slot + s, block_of(h, b, i), 0)
                ),
            ],
            out_specs=[
                pl.BlockSpec((owners, 1, pairs, width), out_map(index)) for index in range(parts)
            ],
            scratch_shapes=[
                pltpu.VMEM((chunk_slots, depth, owners * pairs), received.dtype),
                pltpu.VMEM((width, owners * pairs), jnp.float32),
            ],
        ),
        compiler_params=pltpu.CompilerParams(vmem_limit_bytes=32 * MIB),
        cost_estimate=pl.CostEstimate(
            flops=2 * owners * pairs * chunk_slots * entries * depth,
            bytes_accessed=2 * chunk_slots * entries * depth,
            transcendentals=0,
        ),
    )(int_index, block_mask, received, integrals)


def cycle_kernel(
    owners, parts, place_ref, tiles_ref, first_ref, second_ref, energy_ref, *rest
):
    pieces, (base_ref, dress, wide, rows) = rest[:-4], rest[-4:]
    groups = tiles_ref.shape[2] // LANES
    pairs = tiles_ref.shape[1]
    outer_tile = pl.program_id(0)

    @pl.when(outer_tile == 0)
    def _():
        own = pieces[0].shape[2]
        for owner in range(owners):
            for part in range(parts):
                away = place_ref[1] ^ part
                source = place_ref[0] ^ owner
                block = pieces[0][lax.div(away, len(pieces)), source].astype(jnp.float32)
                for index in range(1, len(pieces)):
                    other = pieces[index][lax.div(away, len(pieces)), source].astype(jnp.float32)
                    block = jnp.where(lax.rem(away, len(pieces)) == index, other, block)
                start = (owner * parts + part) * own
                dress[start : start + own] = block
        low = lax.broadcasted_iota(jnp.int32, (TILE, LANES), 1) < TILE
        for inner in range(VT):
            for couple in range(VT // 2):
                block = dress[
                    inner * TILE : (inner + 1) * TILE, couple * LANES : (couple + 1) * LANES
                ]
                turned = pltpu.roll(block, TILE, 1)
                even = slice(2 * couple * LANES, (2 * couple + 1) * LANES)
                odd = slice((2 * couple + 1) * LANES, (2 * couple + 2) * LANES)
                upper = slice(inner * LANES, inner * LANES + TILE)
                lower = slice(inner * LANES + TILE, (inner + 1) * LANES)
                wide[upper, even] = jnp.where(low, block, 0.0).astype(wide.dtype)
                wide[upper, odd] = jnp.where(low, turned, 0.0).astype(wide.dtype)
                wide[lower, even] = jnp.where(low, 0.0, turned).astype(wide.dtype)
                wide[lower, odd] = jnp.where(low, 0.0, block).astype(wide.dtype)

    for inner in range(VT):
        tile = tiles_ref[inner].astype(jnp.float32)
        stacked = jnp.concatenate(
            [tile[:, g * LANES : (g + 1) * LANES] for g in range(groups)], axis=0
        )
        rows[:, inner * LANES : (inner + 1) * LANES] = stacked.astype(rows.dtype)
    for outer in range(0, VT, 2):
        span = slice(outer * LANES, (outer + 2) * LANES)
        product = jnp.dot(rows[...], wide[:, span], preferred_element_type=jnp.float32)
        for half in range(2):
            cycle = jnp.concatenate(
                [
                    product[g * pairs : (g + 1) * pairs, half * LANES : (half + 1) * LANES]
                    for g in range(groups)
                ],
                axis=1,
            )
            b = outer + half
            below = energy_ref[...] - first_ref[0] - second_ref[b]
            base_ref[b] = tiles_ref[b].astype(jnp.float32) + cycle / below


def cycle_terms(place, tiles, first, second, pair_energy, pieces, owners, parts):
    count, pairs, share = tiles.shape
    whole = lambda a: pl.BlockSpec(a.shape, lambda i, *_: (0,) * a.ndim)
    return pl.pallas_call(
        lambda *refs: cycle_kernel(owners, parts, *refs),
        out_shape=jax.ShapeDtypeStruct(tiles.shape, jnp.float32),
        grid_spec=pltpu.PrefetchScalarGridSpec(
            num_scalar_prefetch=1,
            grid=(WA,),
            in_specs=[
                pl.BlockSpec((VT, pairs, share), lambda i, *_: (i, 0, 0)),
                pl.BlockSpec((1, 1, share), lambda i, *_: (i, 0, 0)),
                whole(second),
                whole(pair_energy),
            ]
            + [whole(piece) for piece in pieces],
            out_specs=pl.BlockSpec((VT, pairs, share), lambda i, *_: (i, 0, 0)),
            scratch_shapes=[
                pltpu.VMEM((VT * TILE, VT * TILE), jnp.float32),
                pltpu.VMEM((VT * LANES, VT * LANES), tiles.dtype),
                pltpu.VMEM((pairs * share // LANES, VT * LANES), tiles.dtype),
            ],
        ),
        compiler_params=pltpu.CompilerParams(vmem_limit_bytes=48 * MIB),
        cost_estimate=pl.CostEstimate(
            flops=4 * count * pairs * share * VT * TILE,
            bytes_accessed=8 * count * pairs * share,
            transcendentals=0,
        ),
    )(place, tiles, first, second, pair_energy, *pieces)


def finish_kernel(
    chunks, out_tiles_ref, base_ref, first_ref, second_ref, energy_ref, *rest
):
    parts, out_ref, sums = rest[:chunks], rest[-2], rest[-1]
    for chunk, part in enumerate(parts):
        owners, size = part.shape[:2]
        for owner in range(owners):
            for slot in range(size):
                tile = out_tiles_ref[(owner * chunks + chunk) * size + slot]
                below = (
                    energy_ref[...] - first_ref[lax.div(tile, VT)] - second_ref[lax.rem(tile, VT)]
                )
                sums[tile] = base_ref[tile] + part[owner, slot].astype(jnp.float32) / below
    out_ref[...] = jnp.swapaxes(sums[...], 0, 1).astype(out_ref.dtype)


def finish(out_tiles, base, first, second, pair_energy, parts, dtype):
    count, pairs, share = base.shape
    width = min(share, 1024)
    return pl.pallas_call(
        lambda *refs: finish_kernel(len(parts), *refs),
        out_shape=jax.ShapeDtypeStruct((pairs, count, share), dtype),
        grid_spec=pltpu.PrefetchScalarGridSpec(
            num_scalar_prefetch=1,
            grid=(share // width,),
            in_specs=[
                pl.BlockSpec((count, pairs, width), lambda i, _: (0, 0, i)),
                pl.BlockSpec((WA, 1, width), lambda i, _: (0, 0, i)),
                pl.BlockSpec((VT, 1, width), lambda i, _: (0, 0, i)),
                pl.BlockSpec((pairs, 1), lambda i, _: (0, 0)),
            ]
            + [
                pl.BlockSpec(part.shape[:2] + (pairs, width), lambda i, _: (0, 0, 0, i))
                for part in parts
            ],
            out_specs=pl.BlockSpec((pairs, count, width), lambda i, _: (0, 0, i)),
            scratch_shapes=[pltpu.VMEM((count, pairs, width), jnp.float32)],
        ),
        compiler_params=pltpu.CompilerParams(vmem_limit_bytes=56 * MIB),
        cost_estimate=pl.CostEstimate(
            flops=8 * count * pairs * share,
            bytes_accessed=8 * count * pairs * share,
            transcendentals=0,
        ),
    )(out_tiles, base, first, second, pair_energy, *parts)


def exchanges(axis, size, radices):
    steps, reach = [], size
    while reach > 1:
        radix = radices.pop(0) if radices else 4
        radix = radix if reach % radix == 0 else 2
        reach //= radix
        steps.append((axis, size, [reach * m for m in range(1, radix)]))
    return steps


def exchange(block, step):
    axis, size, distances = step
    others = [
        lax.ppermute(block, axis, [(j, j ^ distance) for j in range(size)])
        for distance in distances
    ]
    return [block, *others]


def joined(blocks):
    return jnp.stack(blocks, axis=1).reshape((-1,) + blocks[0].shape[1:])


def solution(mesh):
    owners, parts = mesh.shape["pair"], mesh.shape["int"]

    def shards(
        amps, amp_mask, integrals, block_mask, in_tiles, out_tiles, vir_energy, pair_energy, dressing
    ):
        pairs, tiles, share = amps.shape
        slots = tiles // owners
        chunks = 2 if slots % 2 == 0 else 1
        size = slots // chunks
        strip = share // TILE
        int_index = lax.axis_index("int")

        sent = [prepare_first(in_tiles, amps, amp_mask, owners, chunks)]
        masked, *later = prepare(in_tiles, amps, amp_mask, owners, chunks)
        sent += later

        def exchanged(part):
            return lax.all_to_all(part, "pair", split_axis=0, concat_axis=0, tiled=True)

        rows, columns = dressing.shape
        own = rows // parts
        steps = exchanges("pair", owners, [2, 2])
        gathered = [lax.dynamic_slice_in_dim(dressing, int_index * own, own, 0)[None]]
        together = lax.optimization_barrier
        received, returned = [], []
        if steps:
            gathered = exchange(joined(gathered), steps.pop(0))
            sent[0], gathered = together((sent[0], gathered))
        for c in range(chunks):
            if c:
                received[-1], sent[c] = together((received[-1], sent[c]))
            received.append(exchanged(sent[c]))
        for c in range(chunks):
            if c == 0 and steps:
                gathered = exchange(joined(gathered), steps.pop(0))
            if c == 0:
                received[c], gathered = together((received[c], gathered))
            if c == 0 and steps:
                gathered = exchange(joined(gathered), steps.pop(0))
            terms = ladder(
                int_index.astype(jnp.int32)[None], block_mask, received[c], integrals, c, parts
            )
            if c:
                terms, gathered = together((terms, gathered))
            *others, total = terms
            total = total.astype(jnp.float32)
            for r, other in enumerate(others):
                got = lax.ppermute(
                    other, "int", [(j, (j + 1 + r) % parts) for j in range(parts)]
                )
                total = total + got.astype(jnp.float32)
            total = total.astype(amps.dtype)
            if c == 0:
                received[-1], total = together((received[-1], total))
            else:
                returned[-1], total = together((returned[-1], total))
            returned.append(exchanged(total))

        while steps:
            gathered = exchange(joined(gathered), steps.pop(0))
        returned[0], gathered = together((returned[0], gathered))
        pieces = [joined(gathered)[None]]
        for step in exchanges("int", parts, []):
            pieces = exchange(joined(pieces), step)

        energies = vir_energy.reshape(VT, TILE)
        own_energy = lax.dynamic_slice_in_dim(energies[:WA], int_index * strip, strip, 1)
        first = jnp.repeat(own_energy, TILE, axis=1)[:, None]
        second = jnp.tile(energies, (1, strip))[:, None]
        energy = pair_energy[:, None]
        place = jnp.stack([lax.axis_index("pair"), int_index]).astype(jnp.int32)
        base = cycle_terms(place, masked, first, second, energy, pieces, owners, parts)
        return finish(out_tiles, base, first, second, energy, returned, amps.dtype)

    in_specs = (
        P("pair", None, "int"),
        P("pair", None),
        P("pair", None, "int"),
        P("pair"),
        P(),
        P(),
        P(),
        P("pair"),
        P("pair", None),
    )
    out_specs = P("pair", None, "int")
    return jax.shard_map(shards, mesh=mesh, in_specs=in_specs, out_specs=out_specs, check_vma=False)
```

```python
import jax
import jax.numpy as jnp
from jax import lax
from jax.experimental import pallas as pl
from jax.experimental.pallas import tpu as pltpu
from jax.sharding import PartitionSpec as P

TILE = 64
VT = 16
WA = 4
LANES = 128
MIB = 1 << 20


def selection(tile, tile_count, pairs):
    shape = (pairs, pairs * tile_count)
    column = lax.broadcasted_iota(jnp.int32, shape, 1)
    return column == lax.broadcasted_iota(jnp.int32, shape, 0) * tile_count + tile


def first_kernel(chunks, in_tiles_ref, amps_ref, mask_ref, sent_ref, picks):
    pairs, tile_count, width = amps_ref.shape
    owners, size = sent_ref.shape[:2]

    @pl.when(pl.program_id(0) == 0)
    def _():
        mask = jnp.concatenate([mask_ref[...]] * pairs, axis=1) > 0
        for owner in range(owners):
            for slot in range(size):
                tile = in_tiles_ref[owner * chunks * size + slot]
                row = (owner * size + slot) * pairs
                picked = selection(tile, tile_count, pairs) & mask
                picks[row : row + pairs] = jnp.where(picked, 1.0, 0.0)

    amps = amps_ref[...].reshape(pairs * tile_count, width)
    rows = jnp.dot(picks[...].astype(amps.dtype), amps, preferred_element_type=jnp.float32)
    sent_ref[...] = rows.reshape(sent_ref.shape).astype(sent_ref.dtype)


def prepare_first(in_tiles, amps, amp_mask, owners, chunks):
    pairs, tiles, share = amps.shape
    width = min(share, 1024)
    size = tiles // owners // chunks
    return pl.pallas_call(
        lambda *refs: first_kernel(chunks, *refs),
        out_shape=jax.ShapeDtypeStruct((owners, size, pairs, share), amps.dtype),
        grid_spec=pltpu.PrefetchScalarGridSpec(
            num_scalar_prefetch=1,
            grid=(share // width,),
            in_specs=[
                pl.BlockSpec((pairs, tiles, width), lambda i, _: (0, 0, i)),
                pl.BlockSpec((pairs, tiles), lambda i, _: (0, 0)),
            ],
            out_specs=pl.BlockSpec((owners, size, pairs, width), lambda i, _: (0, 0, 0, i)),
            scratch_shapes=[pltpu.VMEM((owners * size * pairs, pairs * tiles), jnp.float32)],
        ),
        compiler_params=pltpu.CompilerParams(vmem_limit_bytes=56 * MIB),
        cost_estimate=pl.CostEstimate(
            flops=2 * pairs * pairs * tiles * tiles * share // chunks,
            bytes_accessed=3 * pairs * tiles * share,
            transcendentals=0,
        ),
    )(in_tiles, amps, amp_mask)


def prepare_kernel(owners, chunks, in_tiles_ref, amps_ref, mask_ref, tiles_ref, *sent_refs):
    tile_count = amps_ref.shape[1]
    swapped = jnp.swapaxes(amps_ref[...].astype(jnp.float32), 0, 1)
    for tile in range(tile_count):
        kept = jnp.where(mask_ref[:, tile : tile + 1] > 0, swapped[tile], 0.0)
        tiles_ref[tile] = kept.astype(tiles_ref.dtype)
    size = tile_count // owners // chunks
    for chunk, sent_ref in enumerate(sent_refs, start=1):
        for owner in range(owners):
            for slot in range(size):
                source = in_tiles_ref[(owner * chunks + chunk) * size + slot]
                sent_ref[owner, slot] = tiles_ref[source]


def prepare(in_tiles, amps, amp_mask, owners, chunks):
    pairs, tiles, share = amps.shape
    width = min(share, 1024)
    size = tiles // owners // chunks
    return pl.pallas_call(
        lambda *refs: prepare_kernel(owners, chunks, *refs),
        out_shape=(jax.ShapeDtypeStruct((tiles, pairs, share), amps.dtype),)
        + (jax.ShapeDtypeStruct((owners, size, pairs, share), amps.dtype),) * (chunks - 1),
        grid_spec=pltpu.PrefetchScalarGridSpec(
            num_scalar_prefetch=1,
            grid=(share // width,),
            in_specs=[
                pl.BlockSpec((pairs, tiles, width), lambda i, _: (0, 0, i)),
                pl.BlockSpec((pairs, tiles), lambda i, _: (0, 0)),
            ],
            out_specs=[pl.BlockSpec((tiles, pairs, width), lambda i, _: (0, 0, i))]
            + [pl.BlockSpec((owners, size, pairs, width), lambda i, _: (0, 0, 0, i))]
            * (chunks - 1),
        ),
        compiler_params=pltpu.CompilerParams(vmem_limit_bytes=56 * MIB),
        cost_estimate=pl.CostEstimate(
            flops=2 * pairs * tiles * share,
            bytes_accessed=6 * pairs * tiles * share,
            transcendentals=0,
        ),
    )(in_tiles, amps, amp_mask)


def ladder_kernel(first_slot, index_ref, keep_ref, x_ref, w_ref, *rest):
    out_refs, (x_columns, sums) = rest[:-2], rest[-2:]
    part, slot, block = pl.program_id(0), pl.program_id(1), pl.program_id(2)
    depth, rows = x_columns.shape[1:]
    step = min(depth, 256)

    @pl.when((part == 0) & (block == 0))
    def _():
        x = x_ref[:, 0].astype(jnp.float32).reshape(rows, depth)
        x_columns[slot] = x.T.astype(x_columns.dtype)

    for k in range(0, depth, step):
        product = jnp.dot(
            w_ref[0, :, k : k + step],
            x_columns[slot, k : k + step],
            preferred_element_type=jnp.float32,
        )
        sums[...] = product if k == 0 else sums[...] + product
    keep = keep_ref[first_slot + slot] > 0
    product = jnp.where(keep, sums[...].T, 0.0)
    for index, out_ref in enumerate(out_refs):

        @pl.when(part == index)
        def _():
            shape = (out_ref.shape[0], out_ref.shape[2], out_ref.shape[3])
            out_ref[:, 0] = product.reshape(shape).astype(out_ref.dtype)


def ladder(int_index, block_mask, received, integrals, chunk, parts):
    owners, chunk_slots, pairs, depth = received.shape
    entries = integrals.shape[1]
    share = entries // parts
    width = min(share, 2048)
    blocks = share // width
    first_slot = chunk * chunk_slots

    def block_of(part, block, index_ref):
        return lax.rem(index_ref[0] + 1 + part, parts) * blocks + block

    def out_map(index):
        def where(part, slot, block, index_ref, keep_ref):
            at = lambda value, last: jnp.where(
                part == index, value, jnp.where(part < index, 0, last)
            )
            return (0, at(slot, chunk_slots - 1), 0, at(block, blocks - 1))

        return where

    return pl.pallas_call(
        lambda *refs: ladder_kernel(first_slot, *refs),
        out_shape=tuple(
            jax.ShapeDtypeStruct((owners, chunk_slots, pairs, share), received.dtype)
            for _ in range(parts)
        ),
        grid_spec=pltpu.PrefetchScalarGridSpec(
            num_scalar_prefetch=2,
            grid=(parts, chunk_slots, blocks),
            in_specs=[
                pl.BlockSpec((owners, 1, pairs, depth), lambda h, s, b, i, k: (0, s, 0, 0)),
                pl.BlockSpec(
                    (1, width, depth), lambda h, s, b, i, k: (first_slot + s, block_of(h, b, i), 0)
                ),
            ],
            out_specs=[
                pl.BlockSpec((owners, 1, pairs, width), out_map(index)) for index in range(parts)
            ],
            scratch_shapes=[
                pltpu.VMEM((chunk_slots, depth, owners * pairs), received.dtype),
                pltpu.VMEM((width, owners * pairs), jnp.float32),
            ],
        ),
        compiler_params=pltpu.CompilerParams(vmem_limit_bytes=32 * MIB),
        cost_estimate=pl.CostEstimate(
            flops=2 * owners * pairs * chunk_slots * entries * depth,
            bytes_accessed=2 * chunk_slots * entries * depth,
            transcendentals=0,
        ),
    )(int_index, block_mask, received, integrals)


def cycle_kernel(
    owners,
    parts,
    chunks,
    place_ref,
    out_tiles_ref,
    tiles_ref,
    early_ref,
    first_ref,
    rows_ref,
    energy_ref,
    *rest,
):
    pieces, (base_ref, dress, wide, rows, sums, early_picks) = rest[:-6], rest[-6:]
    size = VT * WA // owners // chunks
    outer_tile = pl.program_id(0)
    groups = tiles_ref.shape[2] // LANES
    pairs = tiles_ref.shape[1]

    @pl.when(outer_tile == 0)
    def _():
        own = pieces[0].shape[2]
        for owner in range(owners):
            for part in range(parts):
                away = place_ref[1] ^ part
                source = place_ref[0] ^ owner
                block = pieces[0][lax.div(away, len(pieces)), source].astype(jnp.float32)
                for index in range(1, len(pieces)):
                    other = pieces[index][lax.div(away, len(pieces)), source].astype(jnp.float32)
                    block = jnp.where(lax.rem(away, len(pieces)) == index, other, block)
                start = (owner * parts + part) * own
                dress[start : start + own] = block
        low = lax.broadcasted_iota(jnp.int32, (TILE, LANES), 1) < TILE
        for inner in range(VT):
            for couple in range(VT // 2):
                block = dress[
                    inner * TILE : (inner + 1) * TILE, couple * LANES : (couple + 1) * LANES
                ]
                turned = pltpu.roll(block, TILE, 1)
                even = slice(2 * couple * LANES, (2 * couple + 1) * LANES)
                odd = slice((2 * couple + 1) * LANES, (2 * couple + 2) * LANES)
                upper = slice(inner * LANES, inner * LANES + TILE)
                lower = slice(inner * LANES + TILE, (inner + 1) * LANES)
                wide[upper, even] = jnp.where(low, block, 0.0).astype(wide.dtype)
                wide[upper, odd] = jnp.where(low, turned, 0.0).astype(wide.dtype)
                wide[lower, even] = jnp.where(low, 0.0, turned).astype(wide.dtype)
                wide[lower, odd] = jnp.where(low, 0.0, block).astype(wide.dtype)

    for inner in range(VT):
        tile = tiles_ref[inner].astype(jnp.float32)
        stacked = jnp.concatenate(
            [tile[:, g * LANES : (g + 1) * LANES] for g in range(groups)], axis=0
        )
        rows[:, inner * LANES : (inner + 1) * LANES] = stacked.astype(rows.dtype)
    for outer in range(0, VT, 2):
        span = slice(outer * LANES, (outer + 2) * LANES)
        product = jnp.dot(rows[...], wide[:, span], preferred_element_type=jnp.float32)
        for half in range(2):
            cycle = jnp.concatenate(
                [
                    product[g * pairs : (g + 1) * pairs, half * LANES : (half + 1) * LANES]
                    for g in range(groups)
                ],
                axis=1,
            )
            b = outer + half
            below = energy_ref[...] - first_ref[0] - rows_ref[b : b + 1]
            sums[b] = tiles_ref[b].astype(jnp.float32) + cycle / below

    early = 0.0
    if chunks > 1:
        for owner in range(owners):
            for slot in range(size):
                tile = out_tiles_ref[owner * chunks * size + slot]
                inside = jnp.where(lax.div(tile, VT) == outer_tile, 1.0, 0.0)
                row = (owner * size + slot) * pairs
                picked = selection(lax.rem(tile, VT), VT, pairs)
                early_picks[row : row + pairs] = jnp.where(picked, inside, 0.0)
        early = lax.dot_general(
            early_picks[...].astype(early_ref.dtype),
            early_ref[...],
            (((0,), (0,)), ((), ())),
            preferred_element_type=jnp.float32,
        )
    turned = jnp.swapaxes(sums[...], 0, 1)
    for pair in range(pairs):
        total = turned[pair]
        if chunks > 1:
            below = energy_ref[pair : pair + 1] - first_ref[0] - rows_ref[...]
            total += early[pair * VT : (pair + 1) * VT] / below
        base_ref[pair] = total.astype(base_ref.dtype)


def cycle_terms(place, out_tiles, tiles, early, first, rows, pair_energy, pieces, owners, parts, chunks):
    count, pairs, share = tiles.shape
    whole = lambda a: pl.BlockSpec(a.shape, lambda i, *_: (0,) * a.ndim)
    return pl.pallas_call(
        lambda *refs: cycle_kernel(owners, parts, chunks, *refs),
        out_shape=jax.ShapeDtypeStruct((pairs, count, share), tiles.dtype),
        grid_spec=pltpu.PrefetchScalarGridSpec(
            num_scalar_prefetch=2,
            grid=(WA,),
            in_specs=[
                pl.BlockSpec((VT, pairs, share), lambda i, *_: (i, 0, 0)),
                whole(early),
                pl.BlockSpec((1, 1, share), lambda i, *_: (i, 0, 0)),
                whole(rows),
                whole(pair_energy),
            ]
            + [whole(piece) for piece in pieces],
            out_specs=pl.BlockSpec((pairs, VT, share), lambda i, *_: (0, i, 0)),
            scratch_shapes=[
                pltpu.VMEM((VT * TILE, VT * TILE), jnp.float32),
                pltpu.VMEM((VT * LANES, VT * LANES), tiles.dtype),
                pltpu.VMEM((pairs * share // LANES, VT * LANES), tiles.dtype),
                pltpu.VMEM((VT, pairs, share), jnp.float32),
                pltpu.VMEM((early.shape[0], pairs * VT), jnp.float32),
            ],
        ),
        compiler_params=pltpu.CompilerParams(vmem_limit_bytes=36 * MIB),
        cost_estimate=pl.CostEstimate(
            flops=4 * count * pairs * share * VT * TILE,
            bytes_accessed=8 * count * pairs * share,
            transcendentals=0,
        ),
    )(place, out_tiles, tiles, early, first, rows, pair_energy, *pieces)


def finish_kernel(
    owners, chunks, out_tiles_ref, energy_ref, base_ref, first_ref, rows_ref, last_ref, out_ref, *scratch
):
    turned_ref, picks_ref = scratch
    pairs, count, width = out_ref.shape
    span = pl.ds(pl.multiple_of(pl.program_id(0) * width, width), width)
    size = count // owners // chunks

    @pl.when(pl.program_id(0) == 0)
    def _():
        for owner in range(owners):
            for slot in range(size):
                tile = out_tiles_ref[((owner + 1) * chunks - 1) * size + slot]
                row = (owner * size + slot) * pairs
                picked = selection(tile, count, pairs)
                turned_ref[row : row + pairs] = jnp.where(picked, 1.0, 0.0)
        picks_ref[...] = turned_ref[...].T.astype(picks_ref.dtype)

    ladder = jnp.dot(picks_ref[...], last_ref[:, span], preferred_element_type=jnp.float32)
    for pair in range(pairs):
        for outer in range(count // VT):
            inner = slice(outer * VT, (outer + 1) * VT)
            below = energy_ref[pair] - first_ref[outer, :, span] - rows_ref[:, span]
            start = pair * count + outer * VT
            term = ladder[start : start + VT] / below
            out_ref[pair, inner] = (base_ref[pair, inner, span].astype(jnp.float32) + term).astype(
                out_ref.dtype
            )


def finish(out_tiles, base, first, rows, pair_energy, last, owners, chunks):
    pairs, count, share = base.shape
    width = min(share, 512)
    return pl.pallas_call(
        lambda *refs: finish_kernel(owners, chunks, *refs),
        out_shape=jax.ShapeDtypeStruct((pairs, count, share), base.dtype),
        grid=(share // width,),
        in_specs=[pl.BlockSpec(memory_space=pltpu.SMEM)] * 2
        + [pl.BlockSpec(memory_space=pltpu.VMEM)] * 4,
        out_specs=pl.BlockSpec((pairs, count, width), lambda i: (0, 0, i)),
        scratch_shapes=[
            pltpu.VMEM((last.shape[0], pairs * count), jnp.float32),
            pltpu.VMEM((pairs * count, last.shape[0]), base.dtype),
        ],
        compiler_params=pltpu.CompilerParams(vmem_limit_bytes=16 * MIB),
        cost_estimate=pl.CostEstimate(
            flops=8 * count * pairs * share,
            bytes_accessed=6 * count * pairs * share,
            transcendentals=0,
        ),
    )(out_tiles, pair_energy, base, first, rows, last)


def exchanges(axis, size, radices):
    steps, reach = [], size
    while reach > 1:
        radix = radices.pop(0) if radices else 4
        radix = radix if reach % radix == 0 else 2
        reach //= radix
        steps.append((axis, size, [reach * m for m in range(1, radix)]))
    return steps


def exchange(block, step):
    axis, size, distances = step
    others = [
        lax.ppermute(block, axis, [(j, j ^ distance) for j in range(size)])
        for distance in distances
    ]
    return [block, *others]


def joined(blocks):
    return jnp.stack(blocks, axis=1).reshape((-1,) + blocks[0].shape[1:])


def solution(mesh):
    owners, parts = mesh.shape["pair"], mesh.shape["int"]

    def shards(
        amps, amp_mask, integrals, block_mask, in_tiles, out_tiles, vir_energy, pair_energy, dressing
    ):
        pairs, tiles, share = amps.shape
        slots = tiles // owners
        chunks = 2 if slots % 2 == 0 else 1
        size = slots // chunks
        strip = share // TILE
        int_index = lax.axis_index("int")

        sent = [prepare_first(in_tiles, amps, amp_mask, owners, chunks)]
        masked, *later = prepare(in_tiles, amps, amp_mask, owners, chunks)
        sent += later

        def exchanged(part):
            return lax.all_to_all(part, "pair", split_axis=0, concat_axis=0, tiled=True)

        rows, columns = dressing.shape
        own = rows // parts
        steps = exchanges("pair", owners, [2, 2])
        gathered = [lax.dynamic_slice_in_dim(dressing, int_index * own, own, 0)[None]]
        together = lax.optimization_barrier
        energies = vir_energy.reshape(VT, TILE)
        own_energy = lax.dynamic_slice_in_dim(energies[:WA], int_index * strip, strip, 1)
        first = jnp.repeat(own_energy, TILE, axis=1)[:, None]
        second = jnp.tile(energies, (1, strip))
        received, returned = [], []
        if steps:
            gathered = exchange(joined(gathered), steps.pop(0))
            sent[0], gathered = together((sent[0], gathered))
        for c in range(chunks):
            if c:
                received[-1], sent[c] = together((received[-1], sent[c]))
            received.append(exchanged(sent[c]))
        for c in range(chunks):
            if c == 0 and steps:
                gathered = exchange(joined(gathered), steps.pop(0))
            if c == 0:
                received[c], gathered, first, second = together(
                    (received[c], gathered, first, second)
                )
            if c == 0 and steps:
                gathered = exchange(joined(gathered), steps.pop(0))
            terms = ladder(
                int_index.astype(jnp.int32)[None], block_mask, received[c], integrals, c, parts
            )
            if c:
                terms, gathered = together((terms, gathered))
            *others, total = terms
            total = total.astype(jnp.float32)
            for r, other in enumerate(others):
                got = lax.ppermute(
                    other, "int", [(j, (j + 1 + r) % parts) for j in range(parts)]
                )
                total = total + got.astype(jnp.float32)
            total = total.astype(amps.dtype)
            if c == 0:
                received[-1], total = together((received[-1], total))
            else:
                returned[-1], total = together((returned[-1], total))
            returned.append(exchanged(total))

        while steps:
            gathered = exchange(joined(gathered), steps.pop(0))
        returned[0], gathered = together((returned[0], gathered))
        pieces = [joined(gathered)[None]]
        for step in exchanges("int", parts, []):
            pieces = exchange(joined(pieces), step)

        energy = pair_energy[:, None]
        place = jnp.stack([lax.axis_index("pair"), int_index]).astype(jnp.int32)
        flat = [part.reshape(owners * size * pairs, share) for part in returned]
        base = cycle_terms(
            place,
            out_tiles,
            masked,
            flat[0],
            first,
            second,
            energy,
            pieces,
            owners,
            parts,
            chunks,
        )
        return finish(
            out_tiles, base, first, second, pair_energy, flat[-1], owners, chunks
        )

    in_specs = (
        P("pair", None, "int"),
        P("pair", None),
        P("pair", None, "int"),
        P("pair"),
        P(),
        P(),
        P(),
        P("pair"),
        P("pair", None),
    )
    out_specs = P("pair", None, "int")
    return jax.shard_map(shards, mesh=mesh, in_specs=in_specs, out_specs=out_specs, check_vma=False)
```

```python
import jax
import jax.numpy as jnp
from jax import lax
from jax.experimental import pallas as pl
from jax.experimental.pallas import tpu as pltpu
from jax.sharding import PartitionSpec as P

TILE = 64
VT = 16
WA = 4
LANES = 128
MIB = 1 << 20


def selection(tile, tile_count, pairs):
    shape = (pairs, pairs * tile_count)
    column = lax.broadcasted_iota(jnp.int32, shape, 1)
    return column == lax.broadcasted_iota(jnp.int32, shape, 0) * tile_count + tile


def first_kernel(chunks, in_tiles_ref, amps_ref, mask_ref, sent_ref, picks):
    pairs, tile_count, width = amps_ref.shape
    owners, size = sent_ref.shape[:2]

    @pl.when(pl.program_id(0) == 0)
    def _():
        mask = jnp.concatenate([mask_ref[...]] * pairs, axis=1) > 0
        for owner in range(owners):
            for slot in range(size):
                tile = in_tiles_ref[owner * chunks * size + slot]
                row = (owner * size + slot) * pairs
                picked = selection(tile, tile_count, pairs) & mask
                picks[row : row + pairs] = jnp.where(picked, 1.0, 0.0)

    amps = amps_ref[...].reshape(pairs * tile_count, width)
    rows = jnp.dot(picks[...].astype(amps.dtype), amps, preferred_element_type=jnp.float32)
    sent_ref[...] = rows.reshape(sent_ref.shape).astype(sent_ref.dtype)


def prepare_first(in_tiles, amps, amp_mask, owners, chunks):
    pairs, tiles, share = amps.shape
    width = min(share, 1024)
    size = tiles // owners // chunks
    return pl.pallas_call(
        lambda *refs: first_kernel(chunks, *refs),
        out_shape=jax.ShapeDtypeStruct((owners, size, pairs, share), amps.dtype),
        grid_spec=pltpu.PrefetchScalarGridSpec(
            num_scalar_prefetch=1,
            grid=(share // width,),
            in_specs=[
                pl.BlockSpec((pairs, tiles, width), lambda i, _: (0, 0, i)),
                pl.BlockSpec((pairs, tiles), lambda i, _: (0, 0)),
            ],
            out_specs=pl.BlockSpec((owners, size, pairs, width), lambda i, _: (0, 0, 0, i)),
            scratch_shapes=[pltpu.VMEM((owners * size * pairs, pairs * tiles), jnp.float32)],
        ),
        compiler_params=pltpu.CompilerParams(vmem_limit_bytes=56 * MIB),
        cost_estimate=pl.CostEstimate(
            flops=2 * pairs * pairs * tiles * tiles * share // chunks,
            bytes_accessed=3 * pairs * tiles * share,
            transcendentals=0,
        ),
    )(in_tiles, amps, amp_mask)


def prepare_kernel(owners, chunks, in_tiles_ref, amps_ref, mask_ref, tiles_ref, *sent_refs):
    tile_count = amps_ref.shape[1]
    swapped = jnp.swapaxes(amps_ref[...].astype(jnp.float32), 0, 1)
    for tile in range(tile_count):
        kept = jnp.where(mask_ref[:, tile : tile + 1] > 0, swapped[tile], 0.0)
        tiles_ref[tile] = kept.astype(tiles_ref.dtype)
    size = tile_count // owners // chunks
    for chunk, sent_ref in enumerate(sent_refs, start=1):
        for owner in range(owners):
            for slot in range(size):
                source = in_tiles_ref[(owner * chunks + chunk) * size + slot]
                sent_ref[owner, slot] = tiles_ref[source]


def prepare(in_tiles, amps, amp_mask, owners, chunks):
    pairs, tiles, share = amps.shape
    width = min(share, 1024)
    size = tiles // owners // chunks
    return pl.pallas_call(
        lambda *refs: prepare_kernel(owners, chunks, *refs),
        out_shape=(jax.ShapeDtypeStruct((tiles, pairs, share), amps.dtype),)
        + (jax.ShapeDtypeStruct((owners, size, pairs, share), amps.dtype),) * (chunks - 1),
        grid_spec=pltpu.PrefetchScalarGridSpec(
            num_scalar_prefetch=1,
            grid=(share // width,),
            in_specs=[
                pl.BlockSpec((pairs, tiles, width), lambda i, _: (0, 0, i)),
                pl.BlockSpec((pairs, tiles), lambda i, _: (0, 0)),
            ],
            out_specs=[pl.BlockSpec((tiles, pairs, width), lambda i, _: (0, 0, i))]
            + [pl.BlockSpec((owners, size, pairs, width), lambda i, _: (0, 0, 0, i))]
            * (chunks - 1),
        ),
        compiler_params=pltpu.CompilerParams(vmem_limit_bytes=56 * MIB),
        cost_estimate=pl.CostEstimate(
            flops=2 * pairs * tiles * share,
            bytes_accessed=6 * pairs * tiles * share,
            transcendentals=0,
        ),
    )(in_tiles, amps, amp_mask)


def ladder_kernel(first_slot, index_ref, keep_ref, x_ref, w_ref, *rest):
    out_refs, (x_columns, sums) = rest[:-2], rest[-2:]
    part, slot, block = pl.program_id(0), pl.program_id(1), pl.program_id(2)
    depth, rows = x_columns.shape[1:]
    step = min(depth, 256)

    @pl.when((part == 0) & (block == 0))
    def _():
        x = x_ref[:, 0].astype(jnp.float32).reshape(rows, depth)
        x_columns[slot] = x.T.astype(x_columns.dtype)

    for k in range(0, depth, step):
        product = jnp.dot(
            w_ref[0, :, k : k + step],
            x_columns[slot, k : k + step],
            preferred_element_type=jnp.float32,
        )
        sums[...] = product if k == 0 else sums[...] + product
    keep = keep_ref[first_slot + slot] > 0
    product = jnp.where(keep, sums[...].T, 0.0)
    for index, out_ref in enumerate(out_refs):

        @pl.when(part == index)
        def _():
            shape = (out_ref.shape[0], out_ref.shape[2], out_ref.shape[3])
            out_ref[:, 0] = product.reshape(shape).astype(out_ref.dtype)


def ladder(int_index, block_mask, received, integrals, chunk, parts):
    owners, chunk_slots, pairs, depth = received.shape
    entries = integrals.shape[1]
    share = entries // parts
    width = min(share, 2048)
    blocks = share // width
    first_slot = chunk * chunk_slots

    def block_of(part, block, index_ref):
        return lax.rem(index_ref[0] + 1 + part, parts) * blocks + block

    def out_map(index):
        def where(part, slot, block, index_ref, keep_ref):
            at = lambda value, last: jnp.where(
                part == index, value, jnp.where(part < index, 0, last)
            )
            return (0, at(slot, chunk_slots - 1), 0, at(block, blocks - 1))

        return where

    return pl.pallas_call(
        lambda *refs: ladder_kernel(first_slot, *refs),
        out_shape=tuple(
            jax.ShapeDtypeStruct((owners, chunk_slots, pairs, share), received.dtype)
            for _ in range(parts)
        ),
        grid_spec=pltpu.PrefetchScalarGridSpec(
            num_scalar_prefetch=2,
            grid=(parts, chunk_slots, blocks),
            in_specs=[
                pl.BlockSpec((owners, 1, pairs, depth), lambda h, s, b, i, k: (0, s, 0, 0)),
                pl.BlockSpec(
                    (1, width, depth), lambda h, s, b, i, k: (first_slot + s, block_of(h, b, i), 0)
                ),
            ],
            out_specs=[
                pl.BlockSpec((owners, 1, pairs, width), out_map(index)) for index in range(parts)
            ],
            scratch_shapes=[
                pltpu.VMEM((chunk_slots, depth, owners * pairs), received.dtype),
                pltpu.VMEM((width, owners * pairs), jnp.float32),
            ],
        ),
        compiler_params=pltpu.CompilerParams(vmem_limit_bytes=32 * MIB),
        cost_estimate=pl.CostEstimate(
            flops=2 * owners * pairs * chunk_slots * entries * depth,
            bytes_accessed=2 * chunk_slots * entries * depth,
            transcendentals=0,
        ),
    )(int_index, block_mask, received, integrals)


def cycle_kernel(
    owners,
    parts,
    chunks,
    place_ref,
    out_tiles_ref,
    tiles_ref,
    early_ref,
    first_ref,
    rows_ref,
    energy_ref,
    *rest,
):
    pieces, (base_ref, dress, wide, rows, sums, early_picks) = rest[:-6], rest[-6:]
    size = VT * WA // owners // chunks
    outer_tile = pl.program_id(0)
    groups = tiles_ref.shape[2] // LANES
    pairs = tiles_ref.shape[1]

    @pl.when(outer_tile == 0)
    def _():
        own = pieces[0].shape[2]
        for owner in range(owners):
            for part in range(parts):
                away = place_ref[1] ^ part
                source = place_ref[0] ^ owner
                block = pieces[0][lax.div(away, len(pieces)), source].astype(jnp.float32)
                for index in range(1, len(pieces)):
                    other = pieces[index][lax.div(away, len(pieces)), source].astype(jnp.float32)
                    block = jnp.where(lax.rem(away, len(pieces)) == index, other, block)
                start = (owner * parts + part) * own
                dress[start : start + own] = block
        low = lax.broadcasted_iota(jnp.int32, (TILE, LANES), 1) < TILE
        for inner in range(VT):
            for couple in range(VT // 2):
                block = dress[
                    inner * TILE : (inner + 1) * TILE, couple * LANES : (couple + 1) * LANES
                ]
                turned = pltpu.roll(block, TILE, 1)
                even = slice(2 * couple * LANES, (2 * couple + 1) * LANES)
                odd = slice((2 * couple + 1) * LANES, (2 * couple + 2) * LANES)
                upper = slice(inner * LANES, inner * LANES + TILE)
                lower = slice(inner * LANES + TILE, (inner + 1) * LANES)
                wide[upper, even] = jnp.where(low, block, 0.0).astype(wide.dtype)
                wide[upper, odd] = jnp.where(low, turned, 0.0).astype(wide.dtype)
                wide[lower, even] = jnp.where(low, 0.0, turned).astype(wide.dtype)
                wide[lower, odd] = jnp.where(low, 0.0, block).astype(wide.dtype)

    for inner in range(VT):
        tile = tiles_ref[inner].astype(jnp.float32)
        stacked = jnp.concatenate(
            [tile[:, g * LANES : (g + 1) * LANES] for g in range(groups)], axis=0
        )
        rows[:, inner * LANES : (inner + 1) * LANES] = stacked.astype(rows.dtype)
    for outer in range(0, VT, 2):
        span = slice(outer * LANES, (outer + 2) * LANES)
        product = jnp.dot(rows[...], wide[:, span], preferred_element_type=jnp.float32)
        for half in range(2):
            cycle = jnp.concatenate(
                [
                    product[g * pairs : (g + 1) * pairs, half * LANES : (half + 1) * LANES]
                    for g in range(groups)
                ],
                axis=1,
            )
            b = outer + half
            below = energy_ref[...] - first_ref[0] - rows_ref[b : b + 1]
            sums[b] = tiles_ref[b].astype(jnp.float32) + cycle / below

    early = 0.0
    if chunks > 1:
        for owner in range(owners):
            for slot in range(size):
                tile = out_tiles_ref[owner * chunks * size + slot]
                inside = jnp.where(lax.div(tile, VT) == outer_tile, 1.0, 0.0)
                row = (owner * size + slot) * pairs
                picked = selection(lax.rem(tile, VT), VT, pairs)
                early_picks[row : row + pairs] = jnp.where(picked, inside, 0.0)
        early = lax.dot_general(
            early_picks[...].astype(early_ref.dtype),
            early_ref[...],
            (((0,), (0,)), ((), ())),
            preferred_element_type=jnp.float32,
        )
    turned = jnp.swapaxes(sums[...], 0, 1)
    for pair in range(pairs):
        total = turned[pair]
        if chunks > 1:
            below = energy_ref[pair : pair + 1] - first_ref[0] - rows_ref[...]
            total += early[pair * VT : (pair + 1) * VT] / below
        base_ref[pair] = total.astype(base_ref.dtype)


def cycle_terms(place, out_tiles, tiles, early, first, rows, pair_energy, pieces, owners, parts, chunks):
    count, pairs, share = tiles.shape
    whole = lambda a: pl.BlockSpec(a.shape, lambda i, *_: (0,) * a.ndim)
    return pl.pallas_call(
        lambda *refs: cycle_kernel(owners, parts, chunks, *refs),
        out_shape=jax.ShapeDtypeStruct((pairs, count, share), tiles.dtype),
        grid_spec=pltpu.PrefetchScalarGridSpec(
            num_scalar_prefetch=2,
            grid=(WA,),
            in_specs=[
                pl.BlockSpec((VT, pairs, share), lambda i, *_: (i, 0, 0)),
                whole(early),
                pl.BlockSpec((1, 1, share), lambda i, *_: (i, 0, 0)),
                whole(rows),
                whole(pair_energy),
            ]
            + [whole(piece) for piece in pieces],
            out_specs=pl.BlockSpec((pairs, VT, share), lambda i, *_: (0, i, 0)),
            scratch_shapes=[
                pltpu.VMEM((VT * TILE, VT * TILE), jnp.float32),
                pltpu.VMEM((VT * LANES, VT * LANES), tiles.dtype),
                pltpu.VMEM((pairs * share // LANES, VT * LANES), tiles.dtype),
                pltpu.VMEM((VT, pairs, share), jnp.float32),
                pltpu.VMEM((early.shape[0], pairs * VT), jnp.float32),
            ],
        ),
        compiler_params=pltpu.CompilerParams(vmem_limit_bytes=36 * MIB),
        cost_estimate=pl.CostEstimate(
            flops=4 * count * pairs * share * VT * TILE,
            bytes_accessed=8 * count * pairs * share,
            transcendentals=0,
        ),
    )(place, out_tiles, tiles, early, first, rows, pair_energy, *pieces)


def finish_kernel(
    owners, chunks, out_tiles_ref, energy_ref, base_ref, first_ref, rows_ref, last_ref, out_ref, *scratch
):
    turned_ref, picks_ref = scratch
    pairs, count, width = out_ref.shape
    span = pl.ds(pl.multiple_of(pl.program_id(0) * width, width), width)
    size = count // owners // chunks

    @pl.when(pl.program_id(0) == 0)
    def _():
        for owner in range(owners):
            for slot in range(size):
                tile = out_tiles_ref[((owner + 1) * chunks - 1) * size + slot]
                row = (owner * size + slot) * pairs
                picked = selection(tile, count, pairs)
                turned_ref[row : row + pairs] = jnp.where(picked, 1.0, 0.0)
        picks_ref[...] = turned_ref[...].T.astype(picks_ref.dtype)

    ladder = jnp.dot(picks_ref[...], last_ref[:, span], preferred_element_type=jnp.float32)
    for pair in range(pairs):
        for outer in range(count // VT):
            inner = slice(outer * VT, (outer + 1) * VT)
            below = energy_ref[pair] - first_ref[outer, :, span] - rows_ref[:, span]
            start = pair * count + outer * VT
            term = ladder[start : start + VT] / below
            out_ref[pair, inner] = (base_ref[pair, inner, span].astype(jnp.float32) + term).astype(
                out_ref.dtype
            )


def finish(out_tiles, base, first, rows, pair_energy, last, owners, chunks):
    pairs, count, share = base.shape
    width = min(share, 1024)
    return pl.pallas_call(
        lambda *refs: finish_kernel(owners, chunks, *refs),
        out_shape=jax.ShapeDtypeStruct((pairs, count, share), base.dtype),
        grid=(share // width,),
        in_specs=[pl.BlockSpec(memory_space=pltpu.SMEM)] * 2
        + [pl.BlockSpec(memory_space=pltpu.VMEM)] * 4,
        out_specs=pl.BlockSpec((pairs, count, width), lambda i: (0, 0, i)),
        scratch_shapes=[
            pltpu.VMEM((last.shape[0], pairs * count), jnp.float32),
            pltpu.VMEM((pairs * count, last.shape[0]), base.dtype),
        ],
        compiler_params=pltpu.CompilerParams(vmem_limit_bytes=16 * MIB),
        cost_estimate=pl.CostEstimate(
            flops=8 * count * pairs * share,
            bytes_accessed=6 * count * pairs * share,
            transcendentals=0,
        ),
    )(out_tiles, pair_energy, base, first, rows, last)


def exchanges(axis, size, radices):
    steps, reach = [], size
    while reach > 1:
        radix = radices.pop(0) if radices else 4
        radix = radix if reach % radix == 0 else 2
        reach //= radix
        steps.append((axis, size, [reach * m for m in range(1, radix)]))
    return steps


def exchange(block, step):
    axis, size, distances = step
    others = [
        lax.ppermute(block, axis, [(j, j ^ distance) for j in range(size)])
        for distance in distances
    ]
    return [block, *others]


def joined(blocks):
    return jnp.stack(blocks, axis=1).reshape((-1,) + blocks[0].shape[1:])


def solution(mesh):
    owners, parts = mesh.shape["pair"], mesh.shape["int"]

    def shards(
        amps, amp_mask, integrals, block_mask, in_tiles, out_tiles, vir_energy, pair_energy, dressing
    ):
        pairs, tiles, share = amps.shape
        slots = tiles // owners
        chunks = 2 if slots % 2 == 0 else 1
        size = slots // chunks
        strip = share // TILE
        int_index = lax.axis_index("int")

        sent = [prepare_first(in_tiles, amps, amp_mask, owners, chunks)]
        masked, *later = prepare(in_tiles, amps, amp_mask, owners, chunks)
        sent += later

        def exchanged(part):
            return lax.all_to_all(part, "pair", split_axis=0, concat_axis=0, tiled=True)

        rows, columns = dressing.shape
        own = rows // parts
        steps = exchanges("pair", owners, [2, 2])
        gathered = [lax.dynamic_slice_in_dim(dressing, int_index * own, own, 0)[None]]
        together = lax.optimization_barrier
        energies = vir_energy.reshape(VT, TILE)
        own_energy = lax.dynamic_slice_in_dim(energies[:WA], int_index * strip, strip, 1)
        first = jnp.repeat(own_energy, TILE, axis=1)[:, None]
        second = jnp.tile(energies, (1, strip))
        received, returned = [], []
        if steps:
            gathered = exchange(joined(gathered), steps.pop(0))
            sent[0], gathered = together((sent[0], gathered))
        for c in range(chunks):
            if c:
                received[-1], sent[c] = together((received[-1], sent[c]))
            received.append(exchanged(sent[c]))
        for c in range(chunks):
            if c == 0 and steps:
                gathered = exchange(joined(gathered), steps.pop(0))
            if c == 0:
                received[c], gathered, first, second = together(
                    (received[c], gathered, first, second)
                )
            if c == 0 and steps:
                gathered = exchange(joined(gathered), steps.pop(0))
            terms = ladder(
                int_index.astype(jnp.int32)[None], block_mask, received[c], integrals, c, parts
            )
            if c:
                terms, gathered = together((terms, gathered))
            *others, total = terms
            total = total.astype(jnp.float32)
            for r, other in enumerate(others):
                got = lax.ppermute(
                    other, "int", [(j, (j + 1 + r) % parts) for j in range(parts)]
                )
                total = total + got.astype(jnp.float32)
            total = total.astype(amps.dtype)
            if c == 0:
                received[-1], total = together((received[-1], total))
            else:
                returned[-1], total = together((returned[-1], total))
            returned.append(exchanged(total))

        while steps:
            gathered = exchange(joined(gathered), steps.pop(0))
        returned[0], gathered = together((returned[0], gathered))
        pieces = [joined(gathered)[None]]
        for step in exchanges("int", parts, []):
            pieces = exchange(joined(pieces), step)

        energy = pair_energy[:, None]
        place = jnp.stack([lax.axis_index("pair"), int_index]).astype(jnp.int32)
        flat = [part.reshape(owners * size * pairs, share) for part in returned]
        base = cycle_terms(
            place,
            out_tiles,
            masked,
            flat[0],
            first,
            second,
            energy,
            pieces,
            owners,
            parts,
            chunks,
        )
        return finish(
            out_tiles, base, first, second, pair_energy, flat[-1], owners, chunks
        )

    in_specs = (
        P("pair", None, "int"),
        P("pair", None),
        P("pair", None, "int"),
        P("pair"),
        P(),
        P(),
        P(),
        P("pair"),
        P("pair", None),
    )
    out_specs = P("pair", None, "int")
    return jax.shard_map(shards, mesh=mesh, in_specs=in_specs, out_specs=out_specs, check_vma=False)
```
